32 devices in a mesh: redist: 8 (over y, x, core), rep: 4 (over z).
Axes of the slice: x: 2, y: 2, z: 4, core: 2. Of those that a mesh axis runs over, the one named last changes fastest.
Arguments:
- amplitudes: bfloat16 [4, 128, 1024, 1024], P(None, ('redist', 'rep')), may hold values from -6 to 6
- integrals: bfloat16 [128, 1024, 2, 1024], P(None, 'redist'), may hold values from -0.046875 to 0.046875
- occ_irrep: int32 [128], replicated, may hold values from 0 to 7, as said below
- virt_irrep: int32 [1024], replicated, may hold values from 0 to 7, as said below
Outputs:
- cycle_term: float32 [4, 1024, 2, 1024], P(None, None, None, 'redist')
The draws below stay inside these ranges and needn't reach their ends.
Inputs may be any that keep to these rules, and one draw needn't show every extreme that they name: `occ_irrep`: labels never fall along the orbitals; each of the 8 irreps holds one contiguous range of between n // 16 and 3 * n // 16 orbitals, n being 128 or 1024. `virt_irrep`: labels never fall along the orbitals; each of the 8 irreps holds one contiguous range of between n // 16 and 3 * n // 16 orbitals, n being 128 or 1024.
All inputs are finite; a program needn't handle non-finite values.
Results may differ from the reference program's by a relative error of at most 0.0003.
Values may be sent and summed in bfloat16 or wider, within the bound.
A program may use at most 256 MiB of HBM per device.

```python
import jax
import jax.numpy as jnp
from jax import lax

O = 128
V = 1024
ISLAB = 4
JSLAB = 2


def contiguous_labels(key, count):
    base = jnp.arange(1, 8, dtype=jnp.int32) * count // 8
    jitter = jax.random.randint(key, (7,), -(count // 32), count // 32 + 1, dtype=jnp.int32)
    cuts = base + jitter
    places = jnp.arange(count, dtype=jnp.int32)
    return jnp.sum((places[:, None] >= cuts[None, :]).astype(jnp.int32), axis=1).astype(jnp.int32)


def draw_occ_irrep(key, part):
    return contiguous_labels(jax.random.fold_in(key, 11), O)


def draw_virt_irrep(key, part):
    return contiguous_labels(jax.random.fold_in(key, 23), V)


def level_of(rng, dims, shards, smallest, top_value):
    def one(dim, shards_of):
        steps = jax.random.uniform(jax.random.fold_in(jax.random.fold_in(rng, 6), dim), (shards_of,), jnp.float32, smallest / len(shards), top_value / len(shards))
        return jnp.repeat(jnp.exp(steps), dims[dim] // shards_of).reshape((-1,) + (1,) * (len(dims) - dim - 1))

    gain = one(*shards[0])
    for cut in shards[1:]:
        gain = gain * one(*cut)
    return gain


def noise(own_key, dims, spread, bound, cuts=(), kind=jnp.bfloat16):
    array = spread * jax.random.normal(own_key, dims, jnp.float32)
    if cuts:
        array = array * level_of(own_key, dims, cuts, -0.22, 0.18)
    return jnp.clip(array, -bound, bound).astype(kind)


def setup_inputs(seed: int = 0) -> dict:
    arg_keys = jax.random.split(jax.random.key(seed), 5)
    amplitudes = noise(arg_keys[0], (ISLAB, O, V, V), 1.0, 6.0, ((1, 32),))
    integrals = noise(arg_keys[1], (O, V, JSLAB, V), (O * V // 8) ** -0.5, 0.046875, ((1, 8),))
    occ_irrep = draw_occ_irrep(jax.random.fold_in(arg_keys[4], 71), 0)
    virt_irrep = draw_virt_irrep(jax.random.fold_in(arg_keys[4], 71), 0)
    return dict(amplitudes=amplitudes, integrals=integrals, occ_irrep=occ_irrep, virt_irrep=virt_irrep)


def reference(amplitudes, integrals, occ_irrep, virt_irrep):
    occ_rows = occ_irrep[:ISLAB]
    occ_js = occ_irrep[:JSLAB]
    pair_ac = jnp.bitwise_xor(virt_irrep[:, None], virt_irrep[None, :])
    pair_jb = jnp.bitwise_xor(occ_js[:, None], virt_irrep[None, :])

    def advance(total, k_index):
        amp_slice = lax.dynamic_index_in_dim(amplitudes, k_index, 1, keepdims=False)
        k_label = lax.dynamic_index_in_dim(occ_irrep, k_index, 0, keepdims=False)
        pair_ik = jnp.bitwise_xor(occ_rows, k_label)
        allowed = pair_ik[:, None, None] == pair_ac[None, :, :]
        amp_slice = jnp.where(allowed, amp_slice, jnp.zeros((), amp_slice.dtype))
        int_slice = lax.dynamic_index_in_dim(integrals, k_index, 0, keepdims=False)
        pair_kc = jnp.bitwise_xor(k_label, virt_irrep)
        sym_ok = pair_kc[:, None, None] == pair_jb[None, :, :]
        int_slice = jnp.where(sym_ok, int_slice, jnp.zeros((), int_slice.dtype))
        total = total + jnp.dot(amp_slice.reshape(ISLAB * V, V), int_slice.reshape(V, JSLAB * V), preferred_element_type=jnp.float32)
        return total, None

    total, _ = lax.scan(advance, jnp.zeros((ISLAB * V, JSLAB * V), jnp.float32), jnp.arange(O, dtype=jnp.int32))
    return total.reshape(ISLAB, V, JSLAB, V)
```

```python
import jax
import jax.numpy as jnp
from jax import lax
from jax.sharding import PartitionSpec as P


def fold(array, axis, width):
    size = array.shape[axis]
    total = None
    for start in range(0, size, width):
        piece = lax.slice_in_dim(array, start, min(start + width, size), axis=axis)
        short = width - piece.shape[axis]
        if short:
            pads = [(0, 0, 0)] * array.ndim
            pads[axis] = (0, short, 0)
            piece = lax.pad(piece, jnp.zeros((), array.dtype), pads)
        total = piece if total is None else total + piece
    return total


def unfold(array, axis, size):
    width = array.shape[axis]
    copies = -(-size // width)
    return lax.slice_in_dim(jnp.concatenate([array] * copies, axis=axis), 0, size, axis=axis)


def body(amplitudes, integrals, occ_irrep, virt_irrep):
    n_redist = lax.axis_size("redist")
    n_rep = lax.axis_size("rep")
    dev_index = lax.axis_index("redist")
    rep_index = lax.axis_index("rep")
    i_slab, k_block, virt, _ = amplitudes.shape
    c_block = integrals.shape[1]
    j_slab = integrals.shape[2]
    b_block = virt // n_redist
    width = 3 * virt // 16
    zero = jnp.zeros((), amplitudes.dtype)
    slab_label = occ_irrep[0]

    grouped = integrals.reshape(n_redist, n_rep, k_block, c_block, j_slab, virt)
    mine = lax.dynamic_slice_in_dim(grouped, rep_index, 1, 1)[:, 0]
    k_labels = lax.dynamic_slice_in_dim(
        occ_irrep.reshape(n_redist, n_rep, k_block), rep_index, 1, 1
    )[:, 0]
    c_labels = lax.dynamic_slice_in_dim(virt_irrep, dev_index * c_block, c_block)
    want = k_labels[:, :, None] ^ c_labels[None, None, :] ^ slab_label
    keep = want[:, :, :, None, None] == virt_irrep
    folded = fold(jnp.where(keep, mine, zero), 4, width)
    folded = folded.reshape(n_redist * k_block, c_block, j_slab * width)
    moved = lax.all_to_all(folded, "redist", split_axis=0, concat_axis=1, tiled=True)

    my_k = lax.dynamic_slice_in_dim(occ_irrep, (dev_index * n_rep + rep_index) * k_block, k_block)
    pair = my_k[:, None] ^ virt_irrep[None, :] ^ slab_label
    masked = jnp.where(pair[:, None, :] == virt_irrep[None, :, None], amplitudes, zero)
    amps = fold(masked, 2, width)

    wide = unfold(moved.reshape(k_block, virt, j_slab, width), 3, virt)
    sym = jnp.where(pair[:, :, None, None] == virt_irrep, wide, zero)
    part = lax.dot_general(
        amps, sym, (((1, 3), (0, 1)), ((), ())), preferred_element_type=jnp.float32
    )
    share = lax.psum_scatter(part, "redist", scatter_dimension=3, tiled=True)
    share = lax.psum(share, "rep")

    b_labels = lax.dynamic_slice_in_dim(virt_irrep, dev_index * b_block, b_block)
    out_keep = virt_irrep[:, None, None] == b_labels
    return jnp.where(out_keep, unfold(share, 1, virt), jnp.zeros((), jnp.float32))


def solution(mesh):
    placed = (P(None, ("redist", "rep"), None, None), P(None, "redist", None, None), P(), P())
    return jax.shard_map(
        body, mesh=mesh, in_specs=placed, out_specs=P(None, None, None, "redist"), check_vma=False
    )
```

```python
import functools

import jax
import jax.numpy as jnp
from jax import lax
from jax.experimental import pallas as pl
from jax.experimental.pallas import tpu as pltpu
from jax.sharding import PartitionSpec as P

LANES = 128


def fold(array, axis, width):
    size = array.shape[axis]
    total = None
    for start in range(0, size, width):
        piece = lax.slice_in_dim(array, start, min(start + width, size), axis=axis)
        short = width - piece.shape[axis]
        if short:
            pads = [(0, 0, 0)] * array.ndim
            pads[axis] = (0, short, 0)
            piece = lax.pad(piece, jnp.zeros((), array.dtype), pads)
        total = piece if total is None else total + piece
    return total


def unfold(array, axis, size):
    width = array.shape[axis]
    copies = -(-size // width)
    return lax.slice_in_dim(jnp.concatenate([array] * copies, axis=axis), 0, size, axis=axis)


def spans(j_slab, width):
    found = []
    for j in range(j_slab):
        low = j * width // LANES * LANES
        high = -(-(j + 1) * width // LANES) * LANES
        found.append((low, high, j * width - low))
    return found


def one_hot(virt, width, low, high, shift):
    place = jnp.arange(virt, dtype=jnp.int32) % width + shift
    return (place[:, None] == jnp.arange(high - low, dtype=jnp.int32)).astype(jnp.bfloat16)


def fold_kernel(cuts, _, want_ref, labels_ref, ints_ref, *rest):
    hots, out_ref = rest[:-1], rest[-1]
    keep = jnp.where(want_ref[0] == labels_ref[...], 1.0, 0.0).astype(jnp.bfloat16)
    tiles = [None] * (out_ref.shape[-1] // LANES)
    for j, (low, high, _) in enumerate(cuts):
        sums = jnp.dot(
            ints_ref[0, :, j, :] * keep, hots[j][...], preferred_element_type=jnp.float32
        )
        for tile in range(low // LANES, high // LANES):
            piece = sums[:, tile * LANES - low : (tile + 1) * LANES - low]
            tiles[tile] = piece if tiles[tile] is None else tiles[tile] + piece
    for tile, value in enumerate(tiles):
        out_ref[0, :, tile * LANES : (tile + 1) * LANES] = value.astype(jnp.bfloat16)


def fold_integrals(integrals, want, virt_irrep, rep_index, n_redist, n_rep, k_block, width):
    c_block, j_slab, virt = integrals.shape[1:]
    cuts = spans(j_slab, width)
    hots = [one_hot(virt, width, *cut) for cut in cuts]
    packed = cuts[-1][1]

    def source(d, k, rep):
        return ((d * n_rep + rep[0]) * k_block + k, 0, 0, 0)

    return pl.pallas_call(
        functools.partial(fold_kernel, cuts),
        out_shape=jax.ShapeDtypeStruct((n_redist * k_block, c_block, packed), jnp.bfloat16),
        grid_spec=pltpu.PrefetchScalarGridSpec(
            num_scalar_prefetch=1,
            grid=(n_redist, k_block),
            in_specs=[
                pl.BlockSpec((1, c_block, 1), lambda d, k, rep: (d * k_block + k, 0, 0)),
                pl.BlockSpec((1, virt), lambda d, k, rep: (0, 0)),
                pl.BlockSpec((1, c_block, j_slab, virt), source),
            ]
            + [pl.BlockSpec(hot.shape, lambda d, k, rep: (0, 0)) for hot in hots],
            out_specs=pl.BlockSpec((1, c_block, packed), lambda d, k, rep: (d * k_block + k, 0, 0)),
        ),
        compiler_params=pltpu.CompilerParams(vmem_limit_bytes=32 << 20),
        name="fold_integrals",
    )(rep_index[None], want, virt_irrep[None, :], integrals, *hots)


def contract_kernel(low, high, want_ref, labels_ref, amps_ref, ints_ref, hot_ref, out_ref):
    wide = jnp.dot(
        ints_ref[0, :, low:high], hot_ref[...], preferred_element_type=jnp.float32
    )
    sym = jnp.where(want_ref[0] == labels_ref[...], wide, 0.0).astype(jnp.bfloat16)
    k = pl.program_id(1)
    for i in range(amps_ref.shape[0]):
        part = jnp.dot(amps_ref[i, 0], sym, preferred_element_type=jnp.float32)

        @pl.when(k == 0)
        def _():
            out_ref[i] = part

        @pl.when(k > 0)
        def _():
            out_ref[i] += part


def contract(amps, moved, want, virt_irrep, cut, width):
    i_slab, k_block, _, virt = amps.shape
    low, high, shift = cut
    hot = one_hot(virt, width, low, high, shift).T
    step = min(virt, 512)
    return pl.pallas_call(
        functools.partial(contract_kernel, low, high),
        out_shape=jax.ShapeDtypeStruct((i_slab, width, virt), jnp.float32),
        grid=(virt // step, k_block),
        in_specs=[
            pl.BlockSpec((1, virt, 1), lambda n, k: (k, 0, 0)),
            pl.BlockSpec((1, step), lambda n, k: (0, n)),
            pl.BlockSpec((i_slab, 1, width, virt), lambda n, k: (0, k, 0, 0)),
            pl.BlockSpec((1, virt, moved.shape[2]), lambda n, k: (k, 0, 0)),
            pl.BlockSpec((high - low, step), lambda n, k: (0, n)),
        ],
        out_specs=pl.BlockSpec((i_slab, width, step), lambda n, k: (0, 0, n)),
        compiler_params=pltpu.CompilerParams(vmem_limit_bytes=48 << 20),
        cost_estimate=pl.CostEstimate(
            flops=2 * i_slab * k_block * width * virt * virt,
            bytes_accessed=2 * (amps.size * 2 + moved.size * 2) + 4 * i_slab * width * virt,
            transcendentals=0,
        ),
        name="contract",
    )(want, virt_irrep[None, :], amps, moved, hot)


def body(amplitudes, integrals, occ_irrep, virt_irrep):
    n_redist = lax.axis_size("redist")
    n_rep = lax.axis_size("rep")
    dev_index = lax.axis_index("redist")
    rep_index = lax.axis_index("rep")
    i_slab, k_block, virt, _ = amplitudes.shape
    c_block = integrals.shape[1]
    j_slab = integrals.shape[2]
    b_block = virt // n_redist
    width = 3 * virt // 16
    zero = jnp.zeros((), amplitudes.dtype)
    slab_label = occ_irrep[0]

    k_labels = lax.dynamic_slice_in_dim(
        occ_irrep.reshape(n_redist, n_rep, k_block), rep_index, 1, 1
    ).reshape(n_redist * k_block)
    c_labels = lax.dynamic_slice_in_dim(virt_irrep, dev_index * c_block, c_block)
    want = k_labels[:, None] ^ c_labels[None, :] ^ slab_label
    folded = fold_integrals(
        integrals, want[:, :, None], virt_irrep, rep_index, n_redist, n_rep, k_block, width
    )
    moved = lax.all_to_all(folded, "redist", split_axis=0, concat_axis=1, tiled=True)

    my_k = lax.dynamic_slice_in_dim(occ_irrep, (dev_index * n_rep + rep_index) * k_block, k_block)
    pair = my_k[:, None] ^ virt_irrep[None, :] ^ slab_label
    masked = jnp.where(pair[:, None, :] == virt_irrep[None, :, None], amplitudes, zero)
    amps = fold(masked, 2, width)

    shares = []
    for cut in spans(j_slab, width):
        part = contract(amps, moved, pair[:, :, None], virt_irrep, cut, width)
        share = lax.psum_scatter(part, "redist", scatter_dimension=2, tiled=True)
        shares.append(lax.psum(share, "rep"))
    share = jnp.stack(shares, axis=2)

    b_labels = lax.dynamic_slice_in_dim(virt_irrep, dev_index * b_block, b_block)
    out_keep = virt_irrep[:, None, None] == b_labels
    return jnp.where(out_keep, unfold(share, 1, virt), jnp.zeros((), jnp.float32))


def solution(mesh):
    placed = (P(None, ("redist", "rep"), None, None), P(None, "redist", None, None), P(), P())
    return jax.shard_map(
        body, mesh=mesh, in_specs=placed, out_specs=P(None, None, None, "redist"), check_vma=False
    )
```

```python
import functools

import jax
import jax.numpy as jnp
from jax import lax
from jax.experimental import pallas as pl
from jax.experimental.pallas import tpu as pltpu
from jax.sharding import PartitionSpec as P

LANES = 128


def unfold(array, axis, size):
    width = array.shape[axis]
    copies = -(-size // width)
    return lax.slice_in_dim(jnp.concatenate([array] * copies, axis=axis), 0, size, axis=axis)


def spans(j_slab, width):
    found = []
    for j in range(j_slab):
        low = j * width // LANES * LANES
        high = -(-(j + 1) * width // LANES) * LANES
        found.append((low, high, j * width - low))
    return found


def one_hot(virt, width, low, high, shift):
    place = jnp.arange(virt, dtype=jnp.int32) % width + shift
    return (place[:, None] == jnp.arange(high - low, dtype=jnp.int32)).astype(jnp.bfloat16)


def fold_kernel(cuts, _, want_ref, labels_ref, ints_ref, *rest):
    hots, out_ref = rest[:-1], rest[-1]
    keep = jnp.where(want_ref[0] == labels_ref[...], 1.0, 0.0).astype(jnp.bfloat16)
    tiles = [None] * (out_ref.shape[-1] // LANES)
    for j, (low, high, _) in enumerate(cuts):
        sums = jnp.dot(
            ints_ref[0, :, j, :] * keep, hots[j][...], preferred_element_type=jnp.float32
        )
        for tile in range(low // LANES, high // LANES):
            piece = sums[:, tile * LANES - low : (tile + 1) * LANES - low]
            tiles[tile] = piece if tiles[tile] is None else tiles[tile] + piece
    for tile, value in enumerate(tiles):
        out_ref[0, :, tile * LANES : (tile + 1) * LANES] = value.astype(jnp.bfloat16)


def fold_integrals(integrals, want, virt_irrep, rep_index, sizes, first, count, width):
    n_redist, n_rep, k_block = sizes
    c_block, j_slab, virt = integrals.shape[1:]
    cuts = spans(j_slab, width)
    hots = [one_hot(virt, width, *cut) for cut in cuts]
    packed = cuts[-1][1]

    def source(d, k, rep):
        return ((d * n_rep + rep[0]) * k_block + first + k, 0, 0, 0)

    return pl.pallas_call(
        functools.partial(fold_kernel, cuts),
        out_shape=jax.ShapeDtypeStruct((n_redist * count, c_block, packed), jnp.bfloat16),
        grid_spec=pltpu.PrefetchScalarGridSpec(
            num_scalar_prefetch=1,
            grid=(n_redist, count),
            in_specs=[
                pl.BlockSpec((1, c_block, 1), lambda d, k, rep: (d * k_block + first + k, 0, 0)),
                pl.BlockSpec((1, virt), lambda d, k, rep: (0, 0)),
                pl.BlockSpec((1, c_block, j_slab, virt), source),
            ]
            + [pl.BlockSpec(hot.shape, lambda d, k, rep: (0, 0)) for hot in hots],
            out_specs=pl.BlockSpec((1, c_block, packed), lambda d, k, rep: (d * count + k, 0, 0)),
        ),
        compiler_params=pltpu.CompilerParams(vmem_limit_bytes=32 << 20),
        name="fold_integrals",
    )(rep_index[None], want, virt_irrep[None, :], integrals, *hots)


def fold_amps_kernel(width, want_ref, labels_ref, amps_ref, out_ref):
    virt = amps_ref.shape[2]
    zero = jnp.zeros((), jnp.float32)
    piece = 64
    for low in range(0, width, piece):
        total = None
        for start in range(low, virt, width):
            rows = slice(start, start + piece)
            keep = labels_ref[rows, :] == want_ref[0]
            part = jnp.where(keep, amps_ref[0, 0, rows, :].astype(jnp.float32), zero)
            total = part if total is None else total + part
        out_ref[0, 0, low : low + piece, :] = total.astype(out_ref.dtype)


def fold_amps(amplitudes, want, virt_irrep, width):
    i_slab, k_block, virt, _ = amplitudes.shape
    return pl.pallas_call(
        functools.partial(fold_amps_kernel, width),
        out_shape=jax.ShapeDtypeStruct((i_slab, k_block, width, virt), amplitudes.dtype),
        grid=(i_slab, k_block),
        in_specs=[
            pl.BlockSpec((1, 1, virt), lambda i, k: (k, 0, 0)),
            pl.BlockSpec((virt, 1), lambda i, k: (0, 0)),
            pl.BlockSpec((1, 1, virt, virt), lambda i, k: (i, k, 0, 0)),
        ],
        out_specs=pl.BlockSpec((1, 1, width, virt), lambda i, k: (i, k, 0, 0)),
        compiler_params=pltpu.CompilerParams(vmem_limit_bytes=32 << 20),
        cost_estimate=pl.CostEstimate(
            flops=2 * amplitudes.size, bytes_accessed=2 * amplitudes.size, transcendentals=0
        ),
        name="fold_amps",
    )(want, virt_irrep[:, None], amplitudes)


def contract_kernel(cuts, want_ref, labels_ref, amps_ref, ints_ref, *rest):
    hots, out_ref = rest[:-1], rest[-1]
    i_slab, _, width, virt = amps_ref.shape
    keep = want_ref[0] == labels_ref[...]
    amps = amps_ref[:, 0].reshape(i_slab * width, virt)
    k = pl.program_id(1)
    for j, (low, high, _) in enumerate(cuts):
        wide = jnp.dot(ints_ref[0, :, low:high], hots[j][...], preferred_element_type=jnp.float32)
        sym = jnp.where(keep, wide, 0.0).astype(jnp.bfloat16)
        part = jnp.dot(amps, sym, preferred_element_type=jnp.float32)

        for tile in range(out_ref.shape[0]):
            lanes = slice(tile * LANES, (tile + 1) * LANES)
            for i in range(i_slab):
                block = part[i * width : (i + 1) * width, lanes]

                @pl.when(k == 0)
                def _():
                    out_ref[tile, i, j] = block

                @pl.when(k > 0)
                def _():
                    out_ref[tile, i, j] += block


def contract(amps, moved, want, virt_irrep, cuts, width):
    i_slab, k_block, _, virt = amps.shape
    hots = [one_hot(virt, width, *cut).T for cut in cuts]
    step = min(virt, 512)
    return pl.pallas_call(
        functools.partial(contract_kernel, cuts),
        out_shape=jax.ShapeDtypeStruct(
            (virt // LANES, i_slab, len(cuts), width, LANES), jnp.float32
        ),
        grid=(virt // step, k_block),
        in_specs=[
            pl.BlockSpec((1, virt, 1), lambda n, k: (k, 0, 0)),
            pl.BlockSpec((1, step), lambda n, k: (0, n)),
            pl.BlockSpec((i_slab, 1, width, virt), lambda n, k: (0, k, 0, 0)),
            pl.BlockSpec((1, virt, moved.shape[2]), lambda n, k: (k, 0, 0)),
        ]
        + [pl.BlockSpec((hot.shape[0], step), lambda n, k: (0, n)) for hot in hots],
        out_specs=pl.BlockSpec(
            (step // LANES, i_slab, len(cuts), width, LANES), lambda n, k: (n, 0, 0, 0, 0)
        ),
        compiler_params=pltpu.CompilerParams(vmem_limit_bytes=48 << 20),
        name="contract",
    )(want, virt_irrep[None, :], amps, moved, *hots)


def body(amplitudes, integrals, occ_irrep, virt_irrep):
    n_redist = lax.axis_size("redist")
    n_rep = lax.axis_size("rep")
    dev_index = lax.axis_index("redist")
    rep_index = lax.axis_index("rep")
    i_slab, k_block, virt, _ = amplitudes.shape
    c_block = integrals.shape[1]
    j_slab = integrals.shape[2]
    b_block = virt // n_redist
    width = 3 * virt // 16
    slab_label = occ_irrep[0]

    k_labels = lax.dynamic_slice_in_dim(
        occ_irrep.reshape(n_redist, n_rep, k_block), rep_index, 1, 1
    ).reshape(n_redist * k_block)
    c_labels = lax.dynamic_slice_in_dim(virt_irrep, dev_index * c_block, c_block)
    want = k_labels[:, None] ^ c_labels[None, :] ^ slab_label
    sizes = (n_redist, n_rep, k_block)
    count = max(k_block // 2, 1)
    pieces = []
    for first in range(0, k_block, count):
        folded = fold_integrals(
            integrals, want[:, :, None], virt_irrep, rep_index, sizes, first, count, width
        )
        pieces.append(lax.all_to_all(folded, "redist", split_axis=0, concat_axis=1, tiled=True))
    moved = jnp.concatenate(pieces, axis=0)

    my_k = lax.dynamic_slice_in_dim(occ_irrep, (dev_index * n_rep + rep_index) * k_block, k_block)
    pair = my_k[:, None] ^ virt_irrep[None, :] ^ slab_label
    amps = fold_amps(amplitudes, pair[:, None, :], virt_irrep, width)

    part = contract(amps, moved, pair[:, :, None], virt_irrep, spans(j_slab, width), width)
    if b_block < LANES:
        part = part.reshape(*part.shape[:4], LANES // b_block, b_block)
        part = part.transpose(0, 4, 1, 2, 3, 5)
    part = part.reshape(n_redist * i_slab, j_slab, width, b_block)
    share = lax.psum_scatter(part, ("redist", "rep"), scatter_dimension=0, tiled=True)
    share = lax.all_gather(share, "rep", axis=0, tiled=True).transpose(0, 2, 1, 3)

    b_labels = lax.dynamic_slice_in_dim(virt_irrep, dev_index * b_block, b_block)
    out_keep = virt_irrep[:, None, None] == b_labels
    return jnp.where(out_keep, unfold(share, 1, virt), jnp.zeros((), jnp.float32))


def solution(mesh):
    placed = (P(None, ("redist", "rep"), None, None), P(None, "redist", None, None), P(), P())
    return jax.shard_map(
        body, mesh=mesh, in_specs=placed, out_specs=P(None, None, None, "redist"), check_vma=False
    )
```
